32 devices in a mesh: tile: 2 (over y), gz: 4 (over z), gy: 2 (over x), view: 2 (over core).
Axes of the slice: x: 2, y: 2, z: 4, core: 2. Of those that a mesh axis runs over, the one named last changes fastest.
Arguments:
- images: float32 [6, 128, 128, 128], P('view', ('tile', 'gz'), 'gy'), parts along dimension 1, may hold values from 0.3 to 3
- estimate: float32 [128, 128, 128], P(('tile', 'gz'), 'gy'), parts along dimension 0, may hold values from 0.5 to 2
- psf: float32 [6, 3, 31], P('view'), may hold values from 0.05 to 1
- coverage: int32 [6, 8, 2], P('view', ('tile', 'gz'), 'gy'), parts along dimension 1, may hold values from 0 to 1
Outputs:
- deconvolved: float32 [128, 128, 128], P(('tile', 'gz'), 'gy'), parts along dimension 0
The draws below stay inside these ranges and needn't reach their ends.
There are 2 independent parts, one for each index of `tile`. The reference program is written for one: setup_inputs(seed, part) draws one part's arguments, and reference() takes and returns one part's arrays. A program takes and returns all parts, laid end to end along the dimension named above; an argument that names none is the same for every part. Nothing has to cross between parts.
All inputs are finite; a program needn't handle non-finite values.
Results may differ from the reference program's by a relative error of at most 0.0001.
Values sent between devices are 32-bit elements; how exact they have to be, the bound alone decides.
A program may use at most 64 MiB of HBM per device.

```python
import math
import jax
import jax.numpy as jnp
from jax import lax

CZ = 16
CY = 64
XW = 128
VIEWS = 6
HALF = 15
TAPS = 31
ITERS = 1
ZBLOCKS = 4
YBLOCKS = 2
NZ = 64
NY = 128


def set_ends(values, own_key, low, top_value):
    shape = values.shape
    index_at = [jax.random.randint(jax.random.fold_in(own_key, axis), (), 0, shape[axis]) for axis in range(len(shape))]
    values = values.at[tuple(index_at)].set(low)
    longest = shape.index(max(shape))
    index_at[longest] = (index_at[longest] + 1) % shape[longest]
    return values.at[tuple(index_at)].set(top_value)


def block_scale(stream_key, shape, shards, low, largest):
    level = 1.0
    for position, parts in shards:
        steps = jax.random.uniform(jax.random.fold_in(jax.random.fold_in(stream_key, 6), position), (parts,), jnp.float32, low / len(shards), largest / len(shards))
        level = level * jnp.repeat(jnp.exp(steps), shape[position] // parts).reshape((-1,) + (1,) * (len(shape) - 1 - position))
    return level


def setup_inputs(seed: int = 0, part: int = 0) -> dict:
    arg_keys = jax.random.split(jax.random.key(seed), 5)
    part_keys = jax.random.split(jax.random.fold_in(arg_keys[4], part), 5)
    return {
        "images": jnp.clip(jnp.exp(math.log(3.0) - 2.3025851 * jax.random.uniform(part_keys[0], (VIEWS, NZ, NY, XW), jnp.float32) ** block_scale(part_keys[0], (VIEWS, NZ, NY, XW), ((0, 2), (1, 4), (2, 2)), -0.2, 0.2)), 0.3, 3.0),
        "estimate": jnp.clip(jnp.exp(math.log(2.0) - 1.3862944 * jax.random.uniform(part_keys[1], (NZ, NY, XW), jnp.float32) ** block_scale(part_keys[1], (NZ, NY, XW), ((0, 4), (1, 2)), -0.2, 0.2)), 0.5, 2.0),
        "psf": jnp.clip(jnp.exp(math.log(1.0) - 2.9957323 * jax.random.uniform(arg_keys[2], (VIEWS, 3, TAPS), jnp.float32) ** block_scale(arg_keys[2], (VIEWS, 3, TAPS), ((0, 2),), -0.2, 0.2)), 0.05, 1.0),
        "coverage": set_ends(jax.random.randint(part_keys[3], (VIEWS, ZBLOCKS, YBLOCKS), 0, 2), jax.random.fold_in(part_keys[3], 1), 0, 1).astype(jnp.int32),
    }


def axis_pass(field, taps, axis):
    moved = jnp.moveaxis(field, axis, -1)
    shape = moved.shape
    flat = moved.reshape(-1, 1, shape[-1])
    result = lax.conv_general_dilated(flat, taps.reshape(1, 1, -1).astype(jnp.float32), (1,), [(HALF, HALF)], precision=lax.Precision.HIGHEST)
    return jnp.moveaxis(result.reshape(shape), -1, axis)


def blur_all(field, kernels):
    for axis in range(3):
        field = axis_pass(field, kernels[axis], axis)
    return field


def reference(images, estimate, psf, coverage):
    kernel = psf / jnp.sum(psf, axis=2, keepdims=True)
    cover_mask = jnp.repeat(jnp.repeat(coverage, CZ, axis=1), CY, axis=2)
    field = estimate
    for step in range(ITERS):
        factor = jnp.ones_like(field)
        for view_id in range(VIEWS):
            blurred = blur_all(field, kernel[view_id])
            ratio = images[view_id] / blurred
            correction = blur_all(ratio, kernel[view_id][:, ::-1])
            factor = factor * jnp.where(cover_mask[view_id][:, :, None] > 0, correction, jnp.float32(1.0))
        field = field * factor
    return field
```

```python
import functools

import jax
import jax.numpy as jnp
from jax import lax
from jax.experimental import pallas as pl
from jax.experimental.pallas import tpu as pltpu
from jax.sharding import PartitionSpec as P

HALF = 15
TAPS = 2 * HALF + 1
PAD = HALF + 1
PARTS = 4


def split(value):
    high = value.astype(jnp.bfloat16)
    low = (value - high.astype(jnp.float32)).astype(jnp.bfloat16)
    return high, low


def kernel(sizes, zpeers, ypeers, psf, cov, images_hbm, est_hbm, out,
           fpad, gz_out, images, rpad, cpad, acc, other,
           wzf, wzb, wyf, wyb, wxf, wxb, send, recv, local_sem):
    views, depth, height, width = sizes
    zext, yext = depth + 2 * PAD, height + 2 * PAD
    zi, yi, ci = lax.axis_index("gz"), lax.axis_index("gy"), lax.axis_index("view")
    has = {("gz", 1): zi < zpeers - 1, ("gz", -1): zi > 0,
           ("gy", 1): yi < ypeers - 1, ("gy", -1): yi > 0}
    index = {"gz": zi, "gy": yi}
    sides = ((1, 0), (-1, 1))
    far = {"gz": depth, "gy": height}

    def target(axis, side):
        return {axis: index[axis] + side}

    images_copy = pltpu.make_async_copy(images_hbm, images, local_sem.at[0])
    est_copy = pltpu.make_async_copy(
        est_hbm, fpad.at[pl.ds(PAD, depth), pl.ds(PAD, height), :], local_sem.at[1])
    images_copy.start()
    est_copy.start()

    barrier = pltpu.get_barrier_semaphore()
    for (axis, side), there in has.items():
        @pl.when(there)
        def _(axis=axis, side=side):
            pl.semaphore_signal(barrier, inc=1, device_id=target(axis, side),
                                device_id_type=pl.DeviceIdType.MESH)
    pl.semaphore_signal(barrier, inc=1, device_id={"view": 1 - ci},
                        device_id_type=pl.DeviceIdType.MESH)
    count = 1
    for there in has.values():
        count = count + there.astype(jnp.int32)
    pl.semaphore_wait(barrier, count)

    slots = iter(range(64))

    class Remote:
        def __init__(self, axis, side, src, dst):
            slot = next(slots)
            self.axis, self.side = axis, side
            self.copy = pltpu.make_async_remote_copy(
                src_ref=src, dst_ref=dst, send_sem=send.at[slot], recv_sem=recv.at[slot],
                device_id=target(axis, side), device_id_type=pl.DeviceIdType.MESH)

        def start(self):
            pl.when(has[self.axis, self.side])(self.copy.start)

        def wait_recv(self):
            pl.when(has[self.axis, -self.side])(self.copy.wait_recv)

        def wait_send(self):
            pl.when(has[self.axis, self.side])(self.copy.wait_send)

    zsrc = {1: depth - HALF, -1: 0}
    zdst = {1: 1, -1: PAD + depth}
    ysrc = {1: height - PAD, -1: 0}
    ydst = {1: 0, -1: PAD + height}

    f_z = [Remote("gz", s, est_hbm.at[pl.ds(zsrc[s], HALF)],
                  fpad.at[pl.ds(zdst[s], HALF), pl.ds(PAD, height), :]) for s, _ in sides]
    f_y = [Remote("gy", s, est_hbm.at[:, pl.ds(ysrc[s], PAD), :],
                  fpad.at[pl.ds(PAD, depth), pl.ds(ydst[s], PAD), :]) for s, _ in sides]
    f_c = {zs: [Remote("gy", s, fpad.at[pl.ds(zdst[zs], HALF), pl.ds(PAD + ysrc[s], PAD), :],
                       fpad.at[pl.ds(zdst[zs], HALF), pl.ds(ydst[s], PAD), :]) for s, _ in sides]
           for zs, _ in sides}

    def ratio_halo(v, s, first, rows):
        return Remote("gz", s,
                      rpad.at[v, pl.ds(PAD + zsrc[s], HALF), pl.ds(first, rows), :],
                      rpad.at[v, pl.ds(zdst[s], HALF), pl.ds(first, rows), :])

    r_outer = [[ratio_halo(v, s, first, PAD) for s, _ in sides for first in (0, height - PAD)]
               for v in range(views)]
    r_mid = [[ratio_halo(v, s, PAD, height - 2 * PAD) for s, _ in sides] for v in range(views)]
    c_y = [[Remote("gy", s, cpad.at[v, :, pl.ds(PAD + ysrc[s], PAD), :],
                   cpad.at[v, :, pl.ds(ydst[s], PAD), :]) for s, _ in sides]
           for v in range(views)]

    for c in f_z + f_y:
        c.start()

    for k in (0, zext - 1):
        fpad[k] = jnp.zeros((yext, width), jnp.float32)
        for v in range(views):
            rpad[v, k] = jnp.zeros((height, width), jnp.float32)
    for s, _ in sides:
        @pl.when(jnp.logical_not(has["gz", -s]))
        def _(s=s):
            @pl.loop(0, HALF)
            def _(k):
                fpad[zdst[s] + k] = jnp.zeros((yext, width), jnp.float32)
                for v in range(views):
                    rpad[v, zdst[s] + k] = jnp.zeros((height, width), jnp.float32)

        @pl.when(jnp.logical_not(has["gy", -s]))
        def _(s=s):
            @pl.loop(0, zext)
            def _(k):
                fpad[k, pl.ds(ydst[s], PAD), :] = jnp.zeros((PAD, width), jnp.float32)

            @pl.loop(0, depth)
            def _(k):
                for v in range(views):
                    cpad[v, k, pl.ds(ydst[s], PAD), :] = jnp.zeros((PAD, width), jnp.float32)

    def bands(v, axis, shape, offset):
        def step(t, carry):
            fwd, back = carry
            tap = psf[v, axis, t]
            return (jnp.where(offset == t, tap, fwd), jnp.where(offset == TAPS - 1 - t, tap, back))
        zero = jnp.zeros(shape, jnp.float32)
        fwd, back = lax.fori_loop(0, TAPS, step, (zero, zero))
        total = lax.fori_loop(0, TAPS, lambda t, s: s + psf[v, axis, t], jnp.float32(0.0))
        total = jnp.full(shape, total, jnp.float32)
        return split(fwd / total), split(back / total)

    def banded(rows, ext):
        shape = (rows, 2 * ext)
        row = lax.broadcasted_iota(jnp.int32, shape, 0)
        col = lax.broadcasted_iota(jnp.int32, shape, 1)
        col = jnp.where(col >= ext, col - ext, col)
        return shape, col - row - (PAD - HALF)

    for v in range(views):
        (fh, fl), (bh, bl) = bands(v, 0, *banded(depth, zext))
        wzf[pl.ds(v * depth, depth), :] = fh
        wzf[pl.ds((views + v) * depth, depth), :] = fl
        wzb[v, pl.ds(0, depth), :] = bh
        wzb[v, pl.ds(depth, depth), :] = bl
        (fh, fl), (bh, bl) = bands(v, 1, *banded(height, yext))
        wyf[v, pl.ds(0, height), :] = fh
        wyf[v, pl.ds(height, height), :] = fl
        wyb[v, pl.ds(0, height), :] = bh
        wyb[v, pl.ds(height, height), :] = bl
        shape = (width, width)
        offset = (lax.broadcasted_iota(jnp.int32, shape, 0)
                  - lax.broadcasted_iota(jnp.int32, shape, 1) + HALF)
        (fh, fl), (bh, bl) = bands(v, 2, shape, offset)
        for k in range(2):
            wxf[v, pl.ds(k * width, width), pl.ds(0, width)] = fh
            wxf[v, pl.ds(k * width, width), pl.ds(width, width)] = fl
            wxb[v, pl.ds(k * width, width), pl.ds(0, width)] = bh
            wxb[v, pl.ds(k * width, width), pl.ds(width, width)] = bl

    def left(weights, pieces):
        high, low = split(jnp.concatenate(pieces, axis=1))
        both = jnp.dot(weights, jnp.concatenate([high, low], axis=0),
                       preferred_element_type=jnp.float32)
        half = both.shape[0] // 2
        return both[:half] + both[half:]

    def right(value, weights):
        high, low = split(value)
        both = jnp.dot(jnp.concatenate([high, low], axis=1), weights,
                       preferred_element_type=jnp.float32)
        return both[:, :width] + both[:, width:]

    def z_pass(weights, src, src_first, src_stride, dst, dst_first, dst_stride, planes, first, rows):
        group = 4

        def step(k, carry):
            y = first + k * group
            pieces = [src[pl.ds(src_first + y + j, zext, stride=src_stride), :] for j in range(group)]
            result = left(weights, pieces)
            for j in range(group):
                dst[pl.ds(dst_first + y + j, planes, stride=dst_stride), :] = (
                    result[:, j * width:(j + 1) * width])
            return carry
        lax.fori_loop(0, rows // group, step, 0)

    f2 = fpad.reshape(zext * yext, width)
    g2 = gz_out.reshape(views * depth * yext, width)
    r2 = rpad.reshape(views * zext * height, width)
    c2 = cpad.reshape(views * depth * yext, width)

    def forward_z(first, rows):
        z_pass(wzf[...], f2, 0, yext, g2, 0, yext, views * depth, first, rows)

    def backward_z(v, first, rows):
        z_pass(wzb[v], r2, v * zext * height, height, c2, v * depth * yext + PAD, yext, depth,
               first, rows)

    est_copy.wait()
    for (s, _), c in zip(sides, f_z):
        c.wait_recv()
    for zs, _ in sides:
        @pl.when(has["gz", -zs])
        def _(zs=zs):
            for c in f_c[zs]:
                c.start()
    forward_z(PAD, height)
    for c in f_y:
        c.wait_recv()
    for zs, _ in sides:
        @pl.when(has["gz", -zs])
        def _(zs=zs):
            for c in f_c[zs]:
                c.wait_recv()
    forward_z(0, PAD)
    forward_z(PAD + height, PAD)
    images_copy.wait()

    def ratio(v):
        def step(k, carry):
            z = 2 * k
            along_y = left(wyf[v], [gz_out[v * depth + z + j] for j in range(2)])
            rows = jnp.concatenate([along_y[:, :width], along_y[:, width:]], axis=0)
            blurred = right(rows, wxf[v])
            image = jnp.concatenate([images[v, z], images[v, z + 1]], axis=0)
            result = right(image / blurred, wxb[v])
            rpad[v, PAD + z] = result[:height]
            rpad[v, PAD + z + 1] = result[height:]
            return carry
        lax.fori_loop(0, depth // 2, step, 0)

    def start(group):
        for c in group:
            c.start()

    for v in range(views):
        ratio(v)
        start(r_outer[v])
        if v == 0:
            start(r_mid[v])
    for v in range(1, views):
        start(r_mid[v])

    def correction(v, first, planes):
        covered = jnp.full((height, width), cov[v, 0, 0], jnp.int32) > 0

        def step(k, carry):
            z = first + 2 * k
            result = left(wyb[v], [cpad[v, z + j] for j in range(2)])
            for j in range(2):
                masked = jnp.where(covered, result[:, j * width:(j + 1) * width], jnp.float32(1.0))
                acc[z + j] = masked if v == 0 else acc[z + j] * masked
            return carry
        lax.fori_loop(0, planes // 2, step, 0)

    def outer(v):
        for c in r_outer[v]:
            c.wait_recv()
        backward_z(v, 0, PAD)
        backward_z(v, height - PAD, PAD)
        start(c_y[v])

    def mid(v):
        for c in r_mid[v]:
            c.wait_recv()
        backward_z(v, PAD, height - 2 * PAD)
        for c in c_y[v]:
            c.wait_recv()

    outer(0)
    mid(0)
    correction(0, 0, depth)
    for v in range(1, views):
        outer(v)
    for v in range(1, views - 1):
        mid(v)
        correction(v, 0, depth)
    mid(views - 1)

    per = depth // PARTS
    exchange = []
    for k in range(PARTS):
        correction(views - 1, k * per, per)
        slot = next(slots)
        part = pltpu.make_async_remote_copy(
            src_ref=acc.at[pl.ds(k * per, per)], dst_ref=other.at[pl.ds(k * per, per)],
            send_sem=send.at[slot], recv_sem=recv.at[slot],
            device_id={"view": 1 - ci}, device_id_type=pl.DeviceIdType.MESH)
        part.start()
        exchange.append(part)
    for k, part in enumerate(exchange):
        part.wait_recv()

        def step(z, carry):
            out[z] = fpad[PAD + z, pl.ds(PAD, height), :] * (acc[z] * other[z])
            return carry
        lax.fori_loop(k * per, (k + 1) * per, step, 0)

    for c in f_z + f_y:
        c.wait_send()
    for zs, _ in sides:
        @pl.when(has["gz", -zs])
        def _(zs=zs):
            for c in f_c[zs]:
                c.wait_send()
    for v in range(views):
        for c in r_outer[v] + r_mid[v] + c_y[v]:
            c.wait_send()
    for part in exchange:
        part.wait_send()


def solution(mesh):
    zpeers, ypeers = mesh.shape["gz"], mesh.shape["gy"]

    def body(images, estimate, psf, coverage):
        views, depth, height, width = images.shape
        zext, yext = depth + 2 * PAD, height + 2 * PAD
        f32, bf16 = jnp.float32, jnp.bfloat16
        return pl.pallas_call(
            functools.partial(kernel, images.shape, zpeers, ypeers),
            out_shape=jax.ShapeDtypeStruct(estimate.shape, f32),
            in_specs=[
                pl.BlockSpec(memory_space=pltpu.SMEM),
                pl.BlockSpec(memory_space=pltpu.SMEM),
                pl.BlockSpec(memory_space=pl.ANY),
                pl.BlockSpec(memory_space=pl.ANY),
            ],
            out_specs=pl.BlockSpec(memory_space=pltpu.VMEM),
            scratch_shapes=[
                pltpu.VMEM((zext, yext, width), f32),
                pltpu.VMEM((views * depth, yext, width), f32),
                pltpu.VMEM(images.shape, f32),
                pltpu.VMEM((views, zext, height, width), f32),
                pltpu.VMEM((views, depth, yext, width), f32),
                pltpu.VMEM(estimate.shape, f32),
                pltpu.VMEM(estimate.shape, f32),
                pltpu.VMEM((2 * views * depth, 2 * zext), bf16),
                pltpu.VMEM((views, 2 * depth, 2 * zext), bf16),
                pltpu.VMEM((views, 2 * height, 2 * yext), bf16),
                pltpu.VMEM((views, 2 * height, 2 * yext), bf16),
                pltpu.VMEM((views, 2 * width, 2 * width), bf16),
                pltpu.VMEM((views, 2 * width, 2 * width), bf16),
                pltpu.SemaphoreType.DMA((64,)),
                pltpu.SemaphoreType.DMA((64,)),
                pltpu.SemaphoreType.DMA((2,)),
            ],
            compiler_params=pltpu.CompilerParams(
                collective_id=0, has_side_effects=True, vmem_limit_bytes=40 * 2**20),
        )(psf, coverage, images, estimate)

    return jax.shard_map(
        body,
        mesh=mesh,
        in_specs=(
            P("view", ("tile", "gz"), "gy", None),
            P(("tile", "gz"), "gy", None),
            P("view", None, None),
            P("view", ("tile", "gz"), "gy"),
        ),
        out_specs=P(("tile", "gz"), "gy", None),
        check_vma=False,
    )
```

```python
import functools

import jax
import jax.numpy as jnp
from jax import lax
from jax.experimental import pallas as pl
from jax.experimental.pallas import tpu as pltpu
from jax.sharding import PartitionSpec as P

HALF = 15
TAPS = 2 * HALF + 1
PAD = HALF + 1
PARTS = 4


def split(value):
    high = value.astype(jnp.bfloat16)
    low = (value - high.astype(jnp.float32)).astype(jnp.bfloat16)
    return high, low


def kernel(sizes, zpeers, ypeers, psf, cov, images_hbm, est_hbm, out,
           fpad, gz_out, images, rpad, cpad, acc, other,
           wzf, wzb, wyf, wyb, wym, wyo, wxf, wxb, send, recv, local_sem):
    views, depth, height, width = sizes
    zext, yext = depth + 2 * PAD, height + 2 * PAD
    zi, yi, ci = lax.axis_index("gz"), lax.axis_index("gy"), lax.axis_index("view")
    has = {("gz", 1): zi < zpeers - 1, ("gz", -1): zi > 0,
           ("gy", 1): yi < ypeers - 1, ("gy", -1): yi > 0}
    index = {"gz": zi, "gy": yi}
    sides = ((1, 0), (-1, 1))
    far = {"gz": depth, "gy": height}

    def target(axis, side):
        return {axis: index[axis] + side}

    images_copy = pltpu.make_async_copy(images_hbm, images, local_sem.at[0])
    est_copy = pltpu.make_async_copy(
        est_hbm, fpad.at[pl.ds(PAD, depth), pl.ds(PAD, height), :], local_sem.at[1])
    images_copy.start()
    est_copy.start()

    barrier = pltpu.get_barrier_semaphore()
    for (axis, side), there in has.items():
        @pl.when(there)
        def _(axis=axis, side=side):
            pl.semaphore_signal(barrier, inc=1, device_id=target(axis, side),
                                device_id_type=pl.DeviceIdType.MESH)
    pl.semaphore_signal(barrier, inc=1, device_id={"view": 1 - ci},
                        device_id_type=pl.DeviceIdType.MESH)
    count = 1
    for there in has.values():
        count = count + there.astype(jnp.int32)
    pl.semaphore_wait(barrier, count)

    slots = iter(range(64))

    class Remote:
        def __init__(self, axis, side, src, dst):
            slot = next(slots)
            self.axis, self.side = axis, side
            self.copy = pltpu.make_async_remote_copy(
                src_ref=src, dst_ref=dst, send_sem=send.at[slot], recv_sem=recv.at[slot],
                device_id=target(axis, side), device_id_type=pl.DeviceIdType.MESH)

        def start(self):
            pl.when(has[self.axis, self.side])(self.copy.start)

        def wait_recv(self):
            pl.when(has[self.axis, -self.side])(self.copy.wait_recv)

        def wait_send(self):
            pl.when(has[self.axis, self.side])(self.copy.wait_send)

    class Share:
        def __init__(self, side, ref):
            slot = next(slots)
            self.side = side
            self.copy = pltpu.make_async_remote_copy(
                src_ref=ref, dst_ref=ref, send_sem=send.at[slot], recv_sem=recv.at[slot],
                device_id={"view": 1 - ci}, device_id_type=pl.DeviceIdType.MESH)

        def start(self):
            pl.when(has["gz", -self.side])(self.copy.start)

        def wait_recv(self):
            pl.when(has["gz", -self.side])(self.copy.wait_recv)

        def wait_send(self):
            pl.when(has["gz", -self.side])(self.copy.wait_send)

    zsrc = {1: depth - HALF, -1: 0}
    zdst = {1: 1, -1: PAD + depth}
    ysrc = {1: height - PAD, -1: 0}
    ydst = {1: 0, -1: PAD + height}

    quarter = height // 4
    fetched = (pl.multiple_of(ci * (height - quarter), 8), pl.multiple_of(quarter + ci * quarter, 8))
    f_z = [[Remote("gz", s, est_hbm.at[pl.ds(zsrc[s], HALF), pl.ds(row, quarter), :],
                   fpad.at[pl.ds(zdst[s], HALF), pl.ds(PAD + row, quarter), :]) for s, _ in sides]
           for row in fetched]
    f_s = [[Share(s, fpad.at[pl.ds(zdst[s], HALF), pl.ds(PAD + row, quarter), :]) for s, _ in sides]
           for row in fetched]
    f_y = [Remote("gy", s, est_hbm.at[:, pl.ds(ysrc[s], PAD), :],
                  fpad.at[pl.ds(PAD, depth), pl.ds(ydst[s], PAD), :]) for s, _ in sides]
    f_c = {zs: [Remote("gy", s, fpad.at[pl.ds(zdst[zs], HALF), pl.ds(PAD + ysrc[s], PAD), :],
                       fpad.at[pl.ds(zdst[zs], HALF), pl.ds(ydst[s], PAD), :]) for s, _ in sides]
           for zs, _ in sides}

    def ratio_halo(v, s, first, rows):
        return Remote("gz", s,
                      rpad.at[v, pl.ds(PAD + zsrc[s], HALF), pl.ds(first, rows), :],
                      rpad.at[v, pl.ds(zdst[s], HALF), pl.ds(first, rows), :])

    r_outer = [[ratio_halo(v, s, first, PAD) for s, _ in sides for first in (0, height - PAD)]
               for v in range(views)]
    inner = height - 2 * PAD
    r_mid = [[ratio_halo(v, s, PAD, inner) for s, _ in sides] for v in range(views - 1)]
    r_last = [[ratio_halo(views - 1, s, PAD + k * inner // 2, inner // 2) for s, _ in sides]
              for k in range(2)]
    c_y = [[Remote("gy", s, cpad.at[v, :, pl.ds(PAD + ysrc[s], PAD), :],
                   cpad.at[v, :, pl.ds(ydst[s], PAD), :]) for s, _ in sides]
           for v in range(views)]

    for c in f_z[0] + f_y + f_z[1]:
        c.start()

    for k in (0, zext - 1):
        fpad[k] = jnp.zeros((yext, width), jnp.float32)
        for v in range(views):
            rpad[v, k] = jnp.zeros((height, width), jnp.float32)
    for s, _ in sides:
        @pl.when(jnp.logical_not(has["gz", -s]))
        def _(s=s):
            @pl.loop(0, HALF)
            def _(k):
                fpad[zdst[s] + k] = jnp.zeros((yext, width), jnp.float32)
                for v in range(views):
                    rpad[v, zdst[s] + k] = jnp.zeros((height, width), jnp.float32)

        @pl.when(jnp.logical_not(has["gy", -s]))
        def _(s=s):
            @pl.loop(0, zext)
            def _(k):
                fpad[k, pl.ds(ydst[s], PAD), :] = jnp.zeros((PAD, width), jnp.float32)

            @pl.loop(0, depth)
            def _(k):
                for v in range(views):
                    cpad[v, k, pl.ds(ydst[s], PAD), :] = jnp.zeros((PAD, width), jnp.float32)

    def bands(v, axis, shape, offset):
        def step(t, carry):
            fwd, back, total = carry
            tap = psf[v, axis, t]
            return (jnp.where(offset == t, tap, fwd),
                    jnp.where(offset == TAPS - 1 - t, tap, back), total + tap)
        zero = jnp.zeros(shape, jnp.float32)
        fwd, back, total = lax.fori_loop(0, TAPS, step, (zero, zero, jnp.float32(0.0)), unroll=True)
        total = jnp.full(shape, total, jnp.float32)
        return split(fwd / total), split(back / total)

    def banded(rows, ext):
        shape = (rows, 2 * ext)
        row = lax.broadcasted_iota(jnp.int32, shape, 0)
        col = lax.broadcasted_iota(jnp.int32, shape, 1)
        col = jnp.where(col >= ext, col - ext, col)
        return shape, col - row - (PAD - HALF)

    def z_bands(v):
        (fh, fl), (bh, bl) = bands(v, 0, *banded(depth, zext))
        wzf[pl.ds(v * depth, depth), :] = fh
        wzf[pl.ds((views + v) * depth, depth), :] = fl
        wzb[v, pl.ds(0, depth), :] = bh
        wzb[v, pl.ds(depth, depth), :] = bl

    def y_bands(v):
        (fh, fl), (bh, bl) = bands(v, 1, *banded(height, yext))
        wyb[v, pl.ds(0, height), :] = bh
        wyb[v, pl.ds(height, height), :] = bl
        if v > 0:
            wyf[v, pl.ds(0, height), :] = fh
            wyf[v, pl.ds(height, height), :] = fl

    def x_bands(v):
        shape = (width, width)
        offset = (lax.broadcasted_iota(jnp.int32, shape, 0)
                  - lax.broadcasted_iota(jnp.int32, shape, 1) + HALF)
        (fh, fl), (bh, bl) = bands(v, 2, shape, offset)
        for k in range(2):
            wxf[v, pl.ds(k * width, width), pl.ds(0, width)] = fh
            wxf[v, pl.ds(k * width, width), pl.ds(width, width)] = fl
            wxb[v, pl.ds(k * width, width), pl.ds(0, width)] = bh
            wxb[v, pl.ds(k * width, width), pl.ds(width, width)] = bl

    def part_bands():
        (fh, fl), _ = bands(0, 1, *banded(inner, height))
        wym[pl.ds(0, inner), :] = fh
        wym[pl.ds(inner, inner), :] = fl
        (fh, fl), _ = bands(0, 1, *banded(PAD, 3 * PAD))
        wyo[pl.ds(0, PAD), :] = fh
        wyo[pl.ds(PAD, PAD), :] = fl

    def left(weights, pieces):
        high, low = split(jnp.concatenate(pieces, axis=1))
        both = jnp.dot(weights, jnp.concatenate([high, low], axis=0),
                       preferred_element_type=jnp.float32)
        half = both.shape[0] // 2
        return both[:half] + both[half:]

    def right(value, weights):
        high, low = split(value)
        both = jnp.dot(jnp.concatenate([high, low], axis=1), weights,
                       preferred_element_type=jnp.float32)
        return both[:, :width] + both[:, width:]

    def z_pass(weights, src, src_first, src_stride, dst, dst_first, dst_stride, planes, first, rows):
        group = 8

        def step(k, carry):
            y = first + k * group
            pieces = [src[pl.ds(src_first + y + j, zext, stride=src_stride), :] for j in range(group)]
            result = left(weights, pieces)
            for j in range(group):
                dst[pl.ds(dst_first + y + j, planes, stride=dst_stride), :] = (
                    result[:, j * width:(j + 1) * width])
            return carry
        lax.fori_loop(0, rows // group, step, 0)

    f2 = fpad.reshape(zext * yext, width)
    g2 = gz_out.reshape(views * depth * yext, width)
    r2 = rpad.reshape(views * zext * height, width)
    c2 = cpad.reshape(views * depth * yext, width)

    def forward_z(first, rows):
        z_pass(wzf[...], f2, 0, yext, g2, 0, yext, views * depth, first, rows)

    def backward_z(v, first, rows):
        z_pass(wzb[v], r2, v * zext * height, height, c2, v * depth * yext + PAD, yext, depth,
               first, rows)

    for v in range(views):
        z_bands(v)
    est_copy.wait()
    for k in range(2):
        for c, d in zip(f_z[k], f_s[k]):
            c.wait_recv()
            d.start()
        if k == 0:
            part_bands()
            for d in f_s[0]:
                d.wait_recv()
            for zs, _ in sides:
                @pl.when(has["gz", -zs])
                def _(zs=zs):
                    for c in f_c[zs]:
                        c.start()
            x_bands(0)
    for d in f_s[1]:
        d.wait_recv()
    forward_z(PAD, height)
    images_copy.wait()

    def ratio(v, weights, blocks, first, rows):
        planes = 4

        def step(k, carry):
            z = planes * k
            along_y = left(weights, [gz_out[v * depth + z + j, pl.ds(b, n), :]
                                     for j in range(planes) for b, n in blocks])
            count = planes * len(blocks)
            lines = jnp.concatenate([along_y[:, j * width:(j + 1) * width] for j in range(count)],
                                    axis=0)
            blurred = right(lines, wxf[v])
            image = jnp.concatenate([images[v, z + j, pl.ds(f, rows), :]
                                     for j in range(planes) for f in first], axis=0)
            result = right(image / blurred, wxb[v])
            at = 0
            for j in range(planes):
                for f in first:
                    rpad[v, PAD + z + j, pl.ds(f, rows), :] = result[at:at + rows]
                    at += rows
            return carry
        lax.fori_loop(0, depth // planes, step, 0)

    def start(group):
        for c in group:
            c.start()

    def sent(group):
        for c in group:
            c.wait_send()

    def whole(v):
        ratio(v, wyf[v], [(0, yext)], [0], height)

    ratio(0, wym[...], [(PAD, height)], [PAD], inner)
    start(r_mid[0])
    for c in f_y:
        c.wait_recv()
    for zs, _ in sides:
        @pl.when(has["gz", -zs])
        def _(zs=zs):
            for c in f_c[zs]:
                c.wait_recv()
    forward_z(0, PAD)
    forward_z(PAD + height, PAD)
    ratio(0, wyo[...], [(0, 3 * PAD), (yext - 3 * PAD, 3 * PAD)], [0, height - PAD], PAD)
    start(r_outer[0])
    for v in range(1, views):
        y_bands(v)
        x_bands(v)
        whole(v)
        sent(r_mid[0] if v == 1 else r_outer[v - 2])
        start(r_outer[v])
    y_bands(0)

    def correction(v, first, planes):
        covered = jnp.full((height, width), cov[v, 0, 0], jnp.int32) > 0

        def step(k, carry):
            z = first + 4 * k
            result = left(wyb[v], [cpad[v, z + j] for j in range(4)])
            for j in range(4):
                masked = jnp.where(covered, result[:, j * width:(j + 1) * width], jnp.float32(1.0))
                acc[z + j] = masked if v == 0 else acc[z + j] * masked
            return carry
        lax.fori_loop(0, planes // 4, step, 0)

    def outer(v):
        for c in r_outer[v]:
            c.wait_recv()
        backward_z(v, 0, PAD)
        backward_z(v, height - PAD, PAD)
        start(c_y[v])

    def mid(v):
        for c in r_mid[v]:
            c.wait_recv()
        backward_z(v, PAD, inner)

    def finish(v):
        for c in c_y[v]:
            c.wait_recv()
        correction(v, 0, depth)

    def begin(k):
        pieces = [r_outer[views - 2], r_outer[views - 1]] + r_mid[1:] + r_last
        sent(pieces[k])
        start(pieces[k + 2])

    outer(0)
    mid(0)
    begin(0)
    finish(0)
    for v in range(1, views):
        outer(v)
        if v == 1:
            begin(1)
    for v in range(1, views - 1):
        mid(v)
        begin(v + 1)
        finish(v)
    for k in range(2):
        for c in r_last[k]:
            c.wait_recv()
        backward_z(views - 1, PAD + k * inner // 2, inner // 2)
    for c in c_y[views - 1]:
        c.wait_recv()

    per = depth // PARTS
    exchange = []
    for k in range(PARTS):
        correction(views - 1, k * per, per)
        slot = next(slots)
        part = pltpu.make_async_remote_copy(
            src_ref=acc.at[pl.ds(k * per, per)], dst_ref=other.at[pl.ds(k * per, per)],
            send_sem=send.at[slot], recv_sem=recv.at[slot],
            device_id={"view": 1 - ci}, device_id_type=pl.DeviceIdType.MESH)
        part.start()
        exchange.append(part)
    for k, part in enumerate(exchange):
        part.wait_recv()

        def step(z, carry):
            out[z] = fpad[PAD + z, pl.ds(PAD, height), :] * (acc[z] * other[z])
            return carry
        lax.fori_loop(k * per, (k + 1) * per, step, 0)

    for c in f_z[0] + f_z[1] + f_s[0] + f_s[1] + f_y:
        c.wait_send()
    for zs, _ in sides:
        @pl.when(has["gz", -zs])
        def _(zs=zs):
            for c in f_c[zs]:
                c.wait_send()
    for k in range(2):
        sent(r_last[k])
    for v in range(views):
        sent(c_y[v])
    for part in exchange:
        part.wait_send()


def solution(mesh):
    zpeers, ypeers = mesh.shape["gz"], mesh.shape["gy"]

    def body(images, estimate, psf, coverage):
        views, depth, height, width = images.shape
        zext, yext = depth + 2 * PAD, height + 2 * PAD
        f32, bf16 = jnp.float32, jnp.bfloat16
        return pl.pallas_call(
            functools.partial(kernel, images.shape, zpeers, ypeers),
            out_shape=jax.ShapeDtypeStruct(estimate.shape, f32),
            in_specs=[
                pl.BlockSpec(memory_space=pltpu.SMEM),
                pl.BlockSpec(memory_space=pltpu.SMEM),
                pl.BlockSpec(memory_space=pl.ANY),
                pl.BlockSpec(memory_space=pl.ANY),
            ],
            out_specs=pl.BlockSpec(memory_space=pltpu.VMEM),
            scratch_shapes=[
                pltpu.VMEM((zext, yext, width), f32),
                pltpu.VMEM((views * depth, yext, width), f32),
                pltpu.VMEM(images.shape, f32),
                pltpu.VMEM((views, zext, height, width), f32),
                pltpu.VMEM((views, depth, yext, width), f32),
                pltpu.VMEM(estimate.shape, f32),
                pltpu.VMEM(estimate.shape, f32),
                pltpu.VMEM((2 * views * depth, 2 * zext), bf16),
                pltpu.VMEM((views, 2 * depth, 2 * zext), bf16),
                pltpu.VMEM((views, 2 * height, 2 * yext), bf16),
                pltpu.VMEM((views, 2 * height, 2 * yext), bf16),
                pltpu.VMEM((2 * (height - 2 * PAD), 2 * height), bf16),
                pltpu.VMEM((2 * PAD, 6 * PAD), bf16),
                pltpu.VMEM((views, 2 * width, 2 * width), bf16),
                pltpu.VMEM((views, 2 * width, 2 * width), bf16),
                pltpu.SemaphoreType.DMA((64,)),
                pltpu.SemaphoreType.DMA((64,)),
                pltpu.SemaphoreType.DMA((2,)),
            ],
            compiler_params=pltpu.CompilerParams(
                collective_id=0, has_side_effects=True, vmem_limit_bytes=60 * 2**20),
        )(psf, coverage, images, estimate)

    return jax.shard_map(
        body,
        mesh=mesh,
        in_specs=(
            P("view", ("tile", "gz"), "gy", None),
            P(("tile", "gz"), "gy", None),
            P("view", None, None),
            P("view", ("tile", "gz"), "gy"),
        ),
        out_specs=P(("tile", "gz"), "gy", None),
        check_vma=False,
    )
```

```python
import functools

import jax
import jax.numpy as jnp
from jax import lax
from jax.experimental import pallas as pl
from jax.experimental.pallas import tpu as pltpu
from jax.sharding import PartitionSpec as P

HALF = 15
TAPS = 2 * HALF + 1
PAD = HALF + 1
PARTS = 4


def split(value):
    high = value.astype(jnp.bfloat16)
    low = (value - high.astype(jnp.float32)).astype(jnp.bfloat16)
    return high, low


def kernel(sizes, zpeers, ypeers, psf, cov, images_hbm, est_hbm, out,
           fpad, gz_out, images, rpad, cpad, acc, other,
           wzf, wzb, wyf, wyb, wym, wyo, wxf, wxb, send, recv, local_sem):
    views, depth, height, width = sizes
    zext, yext = depth + 2 * PAD, height + 2 * PAD
    zi, yi, ci = lax.axis_index("gz"), lax.axis_index("gy"), lax.axis_index("view")
    has = {("gz", 1): zi < zpeers - 1, ("gz", -1): zi > 0,
           ("gy", 1): yi < ypeers - 1, ("gy", -1): yi > 0}
    index = {"gz": zi, "gy": yi}
    sides = ((1, 0), (-1, 1))
    far = {"gz": depth, "gy": height}

    def target(axis, side):
        return {axis: index[axis] + side}

    images_copy = pltpu.make_async_copy(images_hbm, images, local_sem.at[0])
    est_copy = pltpu.make_async_copy(
        est_hbm, fpad.at[pl.ds(PAD, depth), pl.ds(PAD, height), :], local_sem.at[1])
    images_copy.start()
    est_copy.start()

    barrier = pltpu.get_barrier_semaphore()
    for (axis, side), there in has.items():
        @pl.when(there)
        def _(axis=axis, side=side):
            pl.semaphore_signal(barrier, inc=1, device_id=target(axis, side),
                                device_id_type=pl.DeviceIdType.MESH)
    pl.semaphore_signal(barrier, inc=1, device_id={"view": 1 - ci},
                        device_id_type=pl.DeviceIdType.MESH)
    count = 1
    for there in has.values():
        count = count + there.astype(jnp.int32)
    pl.semaphore_wait(barrier, count)

    slots = iter(range(64))

    class Remote:
        def __init__(self, axis, side, src, dst):
            slot = next(slots)
            self.axis, self.side = axis, side
            self.copy = pltpu.make_async_remote_copy(
                src_ref=src, dst_ref=dst, send_sem=send.at[slot], recv_sem=recv.at[slot],
                device_id=target(axis, side), device_id_type=pl.DeviceIdType.MESH)

        def start(self):
            pl.when(has[self.axis, self.side])(self.copy.start)

        def wait_recv(self):
            pl.when(has[self.axis, -self.side])(self.copy.wait_recv)

        def wait_send(self):
            pl.when(has[self.axis, self.side])(self.copy.wait_send)

    class Share:
        def __init__(self, side, ref):
            slot = next(slots)
            self.side = side
            self.copy = pltpu.make_async_remote_copy(
                src_ref=ref, dst_ref=ref, send_sem=send.at[slot], recv_sem=recv.at[slot],
                device_id={"view": 1 - ci}, device_id_type=pl.DeviceIdType.MESH)

        def start(self):
            pl.when(has["gz", -self.side])(self.copy.start)

        def wait_recv(self):
            pl.when(has["gz", -self.side])(self.copy.wait_recv)

        def wait_send(self):
            pl.when(has["gz", -self.side])(self.copy.wait_send)

    zsrc = {1: depth - HALF, -1: 0}
    zdst = {1: 1, -1: PAD + depth}
    ysrc = {1: height - PAD, -1: 0}
    ydst = {1: 0, -1: PAD + height}

    quarter = height // 4
    fetched = (pl.multiple_of(ci * (height - quarter), 8), pl.multiple_of(quarter + ci * quarter, 8))
    f_z = [[Remote("gz", s, est_hbm.at[pl.ds(zsrc[s], HALF), pl.ds(row, quarter), :],
                   fpad.at[pl.ds(zdst[s], HALF), pl.ds(PAD + row, quarter), :]) for s, _ in sides]
           for row in fetched]
    f_s = [[Share(s, fpad.at[pl.ds(zdst[s], HALF), pl.ds(PAD + row, quarter), :]) for s, _ in sides]
           for row in fetched]
    f_y = [Remote("gy", s, est_hbm.at[:, pl.ds(ysrc[s], PAD), :],
                  fpad.at[pl.ds(PAD, depth), pl.ds(ydst[s], PAD), :]) for s, _ in sides]
    f_c = {zs: [Remote("gy", s, fpad.at[pl.ds(zdst[zs], HALF), pl.ds(PAD + ysrc[s], PAD), :],
                       fpad.at[pl.ds(zdst[zs], HALF), pl.ds(ydst[s], PAD), :]) for s, _ in sides]
           for zs, _ in sides}

    def ratio_halo(v, s, first, rows):
        return Remote("gz", s,
                      rpad.at[v, pl.ds(PAD + zsrc[s], HALF), pl.ds(first, rows), :],
                      rpad.at[v, pl.ds(zdst[s], HALF), pl.ds(first, rows), :])

    r_outer = [[ratio_halo(v, s, first, PAD) for s, _ in sides for first in (0, height - PAD)]
               for v in range(views)]
    inner = height - 2 * PAD
    r_mid = [[ratio_halo(v, s, PAD, inner) for s, _ in sides] for v in range(views - 1)]
    r_last = [[ratio_halo(views - 1, s, PAD + k * inner // 2, inner // 2) for s, _ in sides]
              for k in range(2)]
    c_y = [[Remote("gy", s, cpad.at[v, :, pl.ds(PAD + ysrc[s], PAD), :],
                   cpad.at[v, :, pl.ds(ydst[s], PAD), :]) for s, _ in sides]
           for v in range(views)]

    for c in f_z[0] + f_y + f_z[1]:
        c.start()

    for k in (0, zext - 1):
        fpad[k] = jnp.zeros((yext, width), jnp.float32)
        for v in range(views):
            rpad[v, k] = jnp.zeros((height, width), jnp.float32)
    for s, _ in sides:
        @pl.when(jnp.logical_not(has["gz", -s]))
        def _(s=s):
            @pl.loop(0, HALF)
            def _(k):
                fpad[zdst[s] + k] = jnp.zeros((yext, width), jnp.float32)
                for v in range(views):
                    rpad[v, zdst[s] + k] = jnp.zeros((height, width), jnp.float32)

        @pl.when(jnp.logical_not(has["gy", -s]))
        def _(s=s):
            @pl.loop(0, zext)
            def _(k):
                fpad[k, pl.ds(ydst[s], PAD), :] = jnp.zeros((PAD, width), jnp.float32)

            @pl.loop(0, depth)
            def _(k):
                for v in range(views):
                    cpad[v, k, pl.ds(ydst[s], PAD), :] = jnp.zeros((PAD, width), jnp.float32)

    def bands(v, axis, shape, offset):
        def step(t, carry):
            fwd, back, total = carry
            tap = psf[v, axis, t]
            return (jnp.where(offset == t, tap, fwd),
                    jnp.where(offset == TAPS - 1 - t, tap, back), total + tap)
        zero = jnp.zeros(shape, jnp.float32)
        fwd, back, total = lax.fori_loop(0, TAPS, step, (zero, zero, jnp.float32(0.0)), unroll=True)
        total = jnp.full(shape, total, jnp.float32)
        return split(fwd / total), split(back / total)

    def banded(rows, ext):
        shape = (rows, 2 * ext)
        row = lax.broadcasted_iota(jnp.int32, shape, 0)
        col = lax.broadcasted_iota(jnp.int32, shape, 1)
        col = jnp.where(col >= ext, col - ext, col)
        return shape, col - row - (PAD - HALF)

    def z_bands(v):
        (fh, fl), (bh, bl) = bands(v, 0, *banded(depth, zext))
        wzf[pl.ds(v * depth, depth), :] = fh
        wzf[pl.ds((views + v) * depth, depth), :] = fl
        wzb[v, pl.ds(0, depth), :] = bh
        wzb[v, pl.ds(depth, depth), :] = bl

    def y_bands(v):
        (fh, fl), (bh, bl) = bands(v, 1, *banded(height, yext))
        wyb[v, pl.ds(0, height), :] = bh
        wyb[v, pl.ds(height, height), :] = bl
        if v > 0:
            wyf[v, pl.ds(0, height), :] = fh
            wyf[v, pl.ds(height, height), :] = fl

    def x_bands(v):
        shape = (width, width)
        offset = (lax.broadcasted_iota(jnp.int32, shape, 0)
                  - lax.broadcasted_iota(jnp.int32, shape, 1) + HALF)
        (fh, fl), (bh, bl) = bands(v, 2, shape, offset)
        for k in range(2):
            wxf[v, pl.ds(k * width, width), pl.ds(0, width)] = fh
            wxf[v, pl.ds(k * width, width), pl.ds(width, width)] = fl
            wxb[v, pl.ds(k * width, width), pl.ds(0, width)] = bh
            wxb[v, pl.ds(k * width, width), pl.ds(width, width)] = bl

    def part_bands():
        (fh, fl), _ = bands(0, 1, *banded(inner, height))
        wym[pl.ds(0, inner), :] = fh
        wym[pl.ds(inner, inner), :] = fl
        (fh, fl), _ = bands(0, 1, *banded(PAD, 3 * PAD))
        wyo[pl.ds(0, PAD), :] = fh
        wyo[pl.ds(PAD, PAD), :] = fl

    def left(weights, pieces):
        high, low = split(jnp.concatenate(pieces, axis=1))
        both = jnp.dot(weights, jnp.concatenate([high, low], axis=0),
                       preferred_element_type=jnp.float32)
        half = both.shape[0] // 2
        return both[:half] + both[half:]

    def right(value, weights):
        high, low = split(value)
        both = jnp.dot(jnp.concatenate([high, low], axis=1), weights,
                       preferred_element_type=jnp.float32)
        return both[:, :width] + both[:, width:]

    def z_pass(weights, src, src_first, src_stride, dst, dst_first, dst_stride, planes, first, rows):
        group = 8

        def step(k, carry):
            y = first + k * group
            pieces = [src[pl.ds(src_first + y + j, zext, stride=src_stride), :] for j in range(group)]
            result = left(weights, pieces)
            for j in range(group):
                dst[pl.ds(dst_first + y + j, planes, stride=dst_stride), :] = (
                    result[:, j * width:(j + 1) * width])
            return carry
        lax.fori_loop(0, rows // group, step, 0)

    f2 = fpad.reshape(zext * yext, width)
    g2 = gz_out.reshape(views * depth * yext, width)
    r2 = rpad.reshape(views * zext * height, width)
    c2 = cpad.reshape(views * depth * yext, width)

    def forward_z(first, rows):
        z_pass(wzf[...], f2, 0, yext, g2, 0, yext, views * depth, first, rows)

    def backward_z(v, first, rows):
        z_pass(wzb[v], r2, v * zext * height, height, c2, v * depth * yext + PAD, yext, depth,
               first, rows)

    for v in range(views):
        z_bands(v)
    part_bands()
    x_bands(0)
    est_copy.wait()
    for k in range(2):
        for c, d in zip(f_z[k], f_s[k]):
            c.wait_recv()
            d.start()
        for d in f_s[k]:
            d.wait_recv()
        if k == 0:
            for zs, _ in sides:
                @pl.when(has["gz", -zs])
                def _(zs=zs):
                    for c in f_c[zs]:
                        c.start()
            forward_z(PAD, quarter)
            forward_z(PAD + height - quarter, quarter)
        else:
            forward_z(PAD + quarter, height - 2 * quarter)
    images_copy.wait()

    def ratio(v, weights, blocks, first, rows):
        planes = 4 * height // (len(first) * rows)

        def step(k, carry):
            z = planes * k
            along_y = left(weights, [gz_out[v * depth + z + j, pl.ds(b, n), :]
                                     for j in range(planes) for b, n in blocks])
            count = planes * len(blocks)
            lines = jnp.concatenate([along_y[:, j * width:(j + 1) * width] for j in range(count)],
                                    axis=0)
            blurred = right(lines, wxf[v])
            image = jnp.concatenate([images[v, z + j, pl.ds(f, rows), :]
                                     for j in range(planes) for f in first], axis=0)
            result = right(image / blurred, wxb[v])
            at = 0
            for j in range(planes):
                for f in first:
                    rpad[v, PAD + z + j, pl.ds(f, rows), :] = result[at:at + rows]
                    at += rows
            return carry
        lax.fori_loop(0, depth // planes, step, 0)

    def start(group):
        for c in group:
            c.start()

    def sent(group):
        for c in group:
            c.wait_send()

    def whole(v):
        ratio(v, wyf[v], [(0, yext)], [0], height)

    ratio(0, wym[...], [(PAD, height)], [PAD], inner)
    start(r_mid[0])
    for c in f_y:
        c.wait_recv()
    for zs, _ in sides:
        @pl.when(has["gz", -zs])
        def _(zs=zs):
            for c in f_c[zs]:
                c.wait_recv()
    forward_z(0, PAD)
    forward_z(PAD + height, PAD)
    ratio(0, wyo[...], [(0, 3 * PAD), (yext - 3 * PAD, 3 * PAD)], [0, height - PAD], PAD)
    start(r_outer[0])
    for v in range(1, views):
        y_bands(v)
        x_bands(v)
        whole(v)
        sent(r_mid[0] if v == 1 else r_outer[v - 2])
        start(r_outer[v])
    y_bands(0)

    def correction(v, first, planes):
        covered = jnp.full((height, width), cov[v], jnp.int32) > 0

        def step(k, carry):
            z = first + 4 * k
            result = left(wyb[v], [cpad[v, z + j] for j in range(4)])
            for j in range(4):
                masked = jnp.where(covered, result[:, j * width:(j + 1) * width], jnp.float32(1.0))
                acc[z + j] = masked if v == 0 else acc[z + j] * masked
            return carry
        lax.fori_loop(0, planes // 4, step, 0)

    def outer(v):
        for c in r_outer[v]:
            c.wait_recv()
        backward_z(v, 0, PAD)
        backward_z(v, height - PAD, PAD)
        start(c_y[v])

    def mid(v):
        for c in r_mid[v]:
            c.wait_recv()
        backward_z(v, PAD, inner)

    def finish(v):
        for c in c_y[v]:
            c.wait_recv()
        correction(v, 0, depth)

    def begin(k):
        pieces = [r_outer[views - 2], r_outer[views - 1]] + r_mid[1:] + r_last
        sent(pieces[k])
        start(pieces[k + 2])

    outer(0)
    mid(0)
    begin(0)
    finish(0)
    for v in range(1, views):
        outer(v)
        if v == 1:
            begin(1)
    for v in range(1, views - 1):
        mid(v)
        begin(v + 1)
        finish(v)
    for k in range(2):
        for c in r_last[k]:
            c.wait_recv()
        backward_z(views - 1, PAD + k * inner // 2, inner // 2)
    for c in c_y[views - 1]:
        c.wait_recv()

    per = depth // PARTS
    exchange = []
    for k in range(PARTS):
        correction(views - 1, k * per, per)
        slot = next(slots)
        part = pltpu.make_async_remote_copy(
            src_ref=acc.at[pl.ds(k * per, per)], dst_ref=other.at[pl.ds(k * per, per)],
            send_sem=send.at[slot], recv_sem=recv.at[slot],
            device_id={"view": 1 - ci}, device_id_type=pl.DeviceIdType.MESH)
        part.start()
        exchange.append(part)
    for k, part in enumerate(exchange):
        part.wait_recv()

        def step(z, carry):
            out[z] = fpad[PAD + z, pl.ds(PAD, height), :] * (acc[z] * other[z])
            return carry
        lax.fori_loop(k * per, (k + 1) * per, step, 0)

    for c in f_z[0] + f_z[1] + f_s[0] + f_s[1] + f_y:
        c.wait_send()
    for zs, _ in sides:
        @pl.when(has["gz", -zs])
        def _(zs=zs):
            for c in f_c[zs]:
                c.wait_send()
    for k in range(2):
        sent(r_last[k])
    for v in range(views):
        sent(c_y[v])
    for part in exchange:
        part.wait_send()


def solution(mesh):
    zpeers, ypeers = mesh.shape["gz"], mesh.shape["gy"]

    def body(images, estimate, psf, coverage):
        views, depth, height, width = images.shape
        zext, yext = depth + 2 * PAD, height + 2 * PAD
        f32, bf16 = jnp.float32, jnp.bfloat16
        return pl.pallas_call(
            functools.partial(kernel, images.shape, zpeers, ypeers),
            out_shape=pltpu.VMEM(estimate.shape, f32),
            in_specs=[
                pl.BlockSpec(memory_space=pltpu.SMEM),
                pl.BlockSpec(memory_space=pltpu.SMEM),
                pl.BlockSpec(memory_space=pl.ANY),
                pl.BlockSpec(memory_space=pl.ANY),
            ],
            out_specs=pl.BlockSpec(memory_space=pltpu.VMEM),
            scratch_shapes=[
                pltpu.VMEM((zext, yext, width), f32),
                pltpu.VMEM((views * depth, yext, width), f32),
                pltpu.VMEM(images.shape, f32),
                pltpu.VMEM((views, zext, height, width), f32),
                pltpu.VMEM((views, depth, yext, width), f32),
                pltpu.VMEM(estimate.shape, f32),
                pltpu.VMEM(estimate.shape, f32),
                pltpu.VMEM((2 * views * depth, 2 * zext), bf16),
                pltpu.VMEM((views, 2 * depth, 2 * zext), bf16),
                pltpu.VMEM((views, 2 * height, 2 * yext), bf16),
                pltpu.VMEM((views, 2 * height, 2 * yext), bf16),
                pltpu.VMEM((2 * (height - 2 * PAD), 2 * height), bf16),
                pltpu.VMEM((2 * PAD, 6 * PAD), bf16),
                pltpu.VMEM((views, 2 * width, 2 * width), bf16),
                pltpu.VMEM((views, 2 * width, 2 * width), bf16),
                pltpu.SemaphoreType.DMA((64,)),
                pltpu.SemaphoreType.DMA((64,)),
                pltpu.SemaphoreType.DMA((2,)),
            ],
            compiler_params=pltpu.CompilerParams(
                collective_id=0, has_side_effects=True, vmem_limit_bytes=60 * 2**20),
        )(psf, coverage.reshape(views), images, estimate)

    return jax.shard_map(
        body,
        mesh=mesh,
        in_specs=(
            P("view", ("tile", "gz"), "gy", None),
            P(("tile", "gz"), "gy", None),
            P("view", None, None),
            P("view", ("tile", "gz"), "gy"),
        ),
        out_specs=P(("tile", "gz"), "gy", None),
        check_vma=False,
    )
```

```python
import functools

import jax
import jax.numpy as jnp
from jax import lax
from jax.experimental import pallas as pl
from jax.experimental.pallas import tpu as pltpu
from jax.sharding import PartitionSpec as P

HALF = 15
TAPS = 2 * HALF + 1
PAD = HALF + 1
PARTS = 4


def split(value):
    high = value.astype(jnp.bfloat16)
    low = (value - high.astype(jnp.float32)).astype(jnp.bfloat16)
    return high, low


def kernel(sizes, zpeers, ypeers, psf, cov, images_hbm, est_hbm, out,
           fpad, gz_out, images, rpad, cpad, acc, other,
           wzf, wzb, wyf, wyb, wym, wyo, wxf, wxb, send, recv, local_sem):
    views, depth, height, width = sizes
    zext, yext = depth + 2 * PAD, height + 2 * PAD
    zi, yi, ci = lax.axis_index("gz"), lax.axis_index("gy"), lax.axis_index("view")
    has = {("gz", 1): zi < zpeers - 1, ("gz", -1): zi > 0,
           ("gy", 1): yi < ypeers - 1, ("gy", -1): yi > 0}
    index = {"gz": zi, "gy": yi}
    sides = ((1, 0), (-1, 1))
    far = {"gz": depth, "gy": height}

    def target(axis, side):
        return {axis: index[axis] + side}

    images_copy = pltpu.make_async_copy(images_hbm, images, local_sem.at[0])
    est_copy = pltpu.make_async_copy(
        est_hbm, fpad.at[pl.ds(PAD, depth), pl.ds(PAD, height), :], local_sem.at[1])
    images_copy.start()
    est_copy.start()

    barrier = pltpu.get_barrier_semaphore()
    for (axis, side), there in has.items():
        @pl.when(there)
        def _(axis=axis, side=side):
            pl.semaphore_signal(barrier, inc=1, device_id=target(axis, side),
                                device_id_type=pl.DeviceIdType.MESH)
    pl.semaphore_signal(barrier, inc=1, device_id={"view": 1 - ci},
                        device_id_type=pl.DeviceIdType.MESH)
    count = 1
    for there in has.values():
        count = count + there.astype(jnp.int32)
    pl.semaphore_wait(barrier, count)

    slots = iter(range(64))

    class Remote:
        def __init__(self, axis, side, src, dst):
            slot = next(slots)
            self.axis, self.side = axis, side
            self.copy = pltpu.make_async_remote_copy(
                src_ref=src, dst_ref=dst, send_sem=send.at[slot], recv_sem=recv.at[slot],
                device_id=target(axis, side), device_id_type=pl.DeviceIdType.MESH)

        def start(self):
            pl.when(has[self.axis, self.side])(self.copy.start)

        def wait_recv(self):
            pl.when(has[self.axis, -self.side])(self.copy.wait_recv)

        def wait_send(self):
            pl.when(has[self.axis, self.side])(self.copy.wait_send)

    class Share:
        def __init__(self, side, ref):
            slot = next(slots)
            self.side = side
            self.copy = pltpu.make_async_remote_copy(
                src_ref=ref, dst_ref=ref, send_sem=send.at[slot], recv_sem=recv.at[slot],
                device_id={"view": 1 - ci}, device_id_type=pl.DeviceIdType.MESH)

        def start(self):
            pl.when(has["gz", -self.side])(self.copy.start)

        def wait_recv(self):
            pl.when(has["gz", -self.side])(self.copy.wait_recv)

        def wait_send(self):
            pl.when(has["gz", -self.side])(self.copy.wait_send)

    zsrc = {1: depth - HALF, -1: 0}
    zdst = {1: 1, -1: PAD + depth}
    ysrc = {1: height - PAD, -1: 0}
    ydst = {1: 0, -1: PAD + height}

    quarter = height // 4
    fetched = (pl.multiple_of(ci * (height - quarter), 8), pl.multiple_of(quarter + ci * quarter, 8))
    f_z = [[Remote("gz", s, est_hbm.at[pl.ds(zsrc[s], HALF), pl.ds(row, quarter), :],
                   fpad.at[pl.ds(zdst[s], HALF), pl.ds(PAD + row, quarter), :]) for s, _ in sides]
           for row in fetched]
    f_s = [[Share(s, fpad.at[pl.ds(zdst[s], HALF), pl.ds(PAD + row, quarter), :]) for s, _ in sides]
           for row in fetched]
    f_y = [Remote("gy", s, est_hbm.at[:, pl.ds(ysrc[s], PAD), :],
                  fpad.at[pl.ds(PAD, depth), pl.ds(ydst[s], PAD), :]) for s, _ in sides]
    f_c = {zs: [Remote("gy", s, fpad.at[pl.ds(zdst[zs], HALF), pl.ds(PAD + ysrc[s], PAD), :],
                       fpad.at[pl.ds(zdst[zs], HALF), pl.ds(ydst[s], PAD), :]) for s, _ in sides]
           for zs, _ in sides}

    def ratio_halo(v, s, first, rows):
        return Remote("gz", s,
                      rpad.at[v, pl.ds(PAD + zsrc[s], HALF), pl.ds(first, rows), :],
                      rpad.at[v, pl.ds(zdst[s], HALF), pl.ds(first, rows), :])

    r_outer = [[ratio_halo(v, s, first, PAD) for s, _ in sides for first in (0, height - PAD)]
               for v in range(views)]
    inner = height - 2 * PAD
    r_mid = [[ratio_halo(v, s, PAD, inner) for s, _ in sides] for v in range(views - 1)]
    r_last = [[ratio_halo(views - 1, s, PAD + k * inner // 2, inner // 2) for s, _ in sides]
              for k in range(2)]
    c_y = [[Remote("gy", s, cpad.at[v, :, pl.ds(PAD + ysrc[s], PAD), :],
                   cpad.at[v, :, pl.ds(ydst[s], PAD), :]) for s, _ in sides]
           for v in range(views)]

    for c in f_z[0] + f_y + f_z[1]:
        c.start()

    for k in (0, zext - 1):
        fpad[k] = jnp.zeros((yext, width), jnp.float32)
        for v in range(views):
            rpad[v, k] = jnp.zeros((height, width), jnp.float32)
    for s, _ in sides:
        @pl.when(jnp.logical_not(has["gz", -s]))
        def _(s=s):
            @pl.loop(0, HALF)
            def _(k):
                fpad[zdst[s] + k] = jnp.zeros((yext, width), jnp.float32)
                for v in range(views):
                    rpad[v, zdst[s] + k] = jnp.zeros((height, width), jnp.float32)

        @pl.when(jnp.logical_not(has["gy", -s]))
        def _(s=s):
            @pl.loop(0, zext)
            def _(k):
                fpad[k, pl.ds(ydst[s], PAD), :] = jnp.zeros((PAD, width), jnp.float32)

            @pl.loop(0, depth)
            def _(k):
                for v in range(views):
                    cpad[v, k, pl.ds(ydst[s], PAD), :] = jnp.zeros((PAD, width), jnp.float32)

    def bands(v, axis, shape, offset):
        def step(t, carry):
            fwd, back, total = carry
            tap = psf[v, axis, t]
            return (jnp.where(offset == t, tap, fwd),
                    jnp.where(offset == TAPS - 1 - t, tap, back), total + tap)
        zero = jnp.zeros(shape, jnp.float32)
        fwd, back, total = lax.fori_loop(0, TAPS, step, (zero, zero, jnp.float32(0.0)), unroll=True)
        total = jnp.full(shape, total, jnp.float32)
        return split(fwd / total), split(back / total)

    def banded(rows, ext):
        shape = (rows, 2 * ext)
        row = lax.broadcasted_iota(jnp.int32, shape, 0)
        col = lax.broadcasted_iota(jnp.int32, shape, 1)
        col = jnp.where(col >= ext, col - ext, col)
        return shape, col - row - (PAD - HALF)

    def z_bands(v):
        (fh, fl), (bh, bl) = bands(v, 0, *banded(depth, zext))
        wzf[pl.ds(v * depth, depth), :] = fh
        wzf[pl.ds((views + v) * depth, depth), :] = fl
        wzb[v, pl.ds(0, depth), :] = bh
        wzb[v, pl.ds(depth, depth), :] = bl

    def y_bands(v):
        (fh, fl), (bh, bl) = bands(v, 1, *banded(height, yext))
        wyb[v, pl.ds(0, height), :] = bh
        wyb[v, pl.ds(height, height), :] = bl
        if v > 0:
            wyf[v, pl.ds(0, height), :] = fh
            wyf[v, pl.ds(height, height), :] = fl

    def x_bands(v):
        shape = (width, width)
        offset = (lax.broadcasted_iota(jnp.int32, shape, 0)
                  - lax.broadcasted_iota(jnp.int32, shape, 1) + HALF)
        (fh, fl), (bh, bl) = bands(v, 2, shape, offset)
        for k in range(2):
            wxf[v, pl.ds(k * width, width), pl.ds(0, width)] = fh
            wxf[v, pl.ds(k * width, width), pl.ds(width, width)] = fl
            wxb[v, pl.ds(k * width, width), pl.ds(0, width)] = bh
            wxb[v, pl.ds(k * width, width), pl.ds(width, width)] = bl

    def part_bands():
        (fh, fl), _ = bands(0, 1, *banded(inner, height))
        wym[pl.ds(0, inner), :] = fh
        wym[pl.ds(inner, inner), :] = fl
        (fh, fl), _ = bands(0, 1, *banded(PAD, 3 * PAD))
        wyo[pl.ds(0, PAD), :] = fh
        wyo[pl.ds(PAD, PAD), :] = fl

    def left(weights, pieces):
        high, low = split(jnp.concatenate(pieces, axis=1))
        both = jnp.dot(weights, jnp.concatenate([high, low], axis=0),
                       preferred_element_type=jnp.float32)
        half = both.shape[0] // 2
        return both[:half] + both[half:]

    def right(value, weights):
        high, low = split(value)
        both = jnp.dot(jnp.concatenate([high, low], axis=1), weights,
                       preferred_element_type=jnp.float32)
        return both[:, :width] + both[:, width:]

    def z_pass(weights, src, src_first, src_stride, dst, dst_first, dst_stride, planes, first, rows):
        group = 8

        def step(k, carry):
            y = first + k * group
            pieces = [src[pl.ds(src_first + y + j, zext, stride=src_stride), :] for j in range(group)]
            result = left(weights, pieces)
            for j in range(group):
                dst[pl.ds(dst_first + y + j, planes, stride=dst_stride), :] = (
                    result[:, j * width:(j + 1) * width])
            return carry
        lax.fori_loop(0, rows // group, step, 0)

    f2 = fpad.reshape(zext * yext, width)
    g2 = gz_out.reshape(views * depth * yext, width)
    r2 = rpad.reshape(views * zext * height, width)
    c2 = cpad.reshape(views * depth * yext, width)

    def forward_z(first, rows):
        z_pass(wzf[...], f2, 0, yext, g2, 0, yext, views * depth, first, rows)

    def backward_z(v, first, rows):
        z_pass(wzb[v], r2, v * zext * height, height, c2, v * depth * yext + PAD, yext, depth,
               first, rows)

    for v in range(views):
        z_bands(v)
    part_bands()
    x_bands(0)
    est_copy.wait()
    for k in range(2):
        for c, d in zip(f_z[k], f_s[k]):
            c.wait_recv()
            d.start()
        for d in f_s[k]:
            d.wait_recv()
        if k == 0:
            for zs, _ in sides:
                @pl.when(has["gz", -zs])
                def _(zs=zs):
                    for c in f_c[zs]:
                        c.start()
            forward_z(PAD, quarter)
            forward_z(PAD + height - quarter, quarter)
        else:
            forward_z(PAD + quarter, height - 2 * quarter)
    images_copy.wait()

    def ratio(v, weights, blocks, first, rows):
        planes = 4 * height // (len(first) * rows)

        def step(k, carry):
            z = planes * k
            along_y = left(weights, [gz_out[v * depth + z + j, pl.ds(b, n), :]
                                     for j in range(planes) for b, n in blocks])
            count = planes * len(blocks)
            lines = jnp.concatenate([along_y[:, j * width:(j + 1) * width] for j in range(count)],
                                    axis=0)
            blurred = right(lines, wxf[v])
            image = jnp.concatenate([images[v, z + j, pl.ds(f, rows), :]
                                     for j in range(planes) for f in first], axis=0)
            result = right(image / blurred, wxb[v])
            at = 0
            for j in range(planes):
                for f in first:
                    rpad[v, PAD + z + j, pl.ds(f, rows), :] = result[at:at + rows]
                    at += rows
            return carry
        lax.fori_loop(0, depth // planes, step, 0, unroll=2)

    def start(group):
        for c in group:
            c.start()

    def sent(group):
        for c in group:
            c.wait_send()

    def whole(v):
        ratio(v, wyf[v], [(0, yext)], [0], height)

    ratio(0, wym[...], [(PAD, height)], [PAD], inner)
    start(r_mid[0])
    for c in f_y:
        c.wait_recv()
    for zs, _ in sides:
        @pl.when(has["gz", -zs])
        def _(zs=zs):
            for c in f_c[zs]:
                c.wait_recv()
    forward_z(0, PAD)
    forward_z(PAD + height, PAD)
    ratio(0, wyo[...], [(0, 3 * PAD), (yext - 3 * PAD, 3 * PAD)], [0, height - PAD], PAD)
    start(r_outer[0])
    for v in range(1, views):
        y_bands(v)
        x_bands(v)
        whole(v)
        sent(r_mid[0] if v == 1 else r_outer[v - 2])
        start(r_outer[v])
    y_bands(0)

    def correction(v, first, planes):
        covered = jnp.full((height, width), cov[v], jnp.int32) > 0

        def step(k, carry):
            z = first + 4 * k
            result = left(wyb[v], [cpad[v, z + j] for j in range(4)])
            for j in range(4):
                masked = jnp.where(covered, result[:, j * width:(j + 1) * width], jnp.float32(1.0))
                acc[z + j] = masked if v == 0 else acc[z + j] * masked
            return carry
        lax.fori_loop(0, planes // 4, step, 0)

    def outer(v):
        for c in r_outer[v]:
            c.wait_recv()
        backward_z(v, 0, PAD)
        backward_z(v, height - PAD, PAD)
        start(c_y[v])

    def mid(v):
        for c in r_mid[v]:
            c.wait_recv()
        backward_z(v, PAD, inner)

    def finish(v):
        for c in c_y[v]:
            c.wait_recv()
        correction(v, 0, depth)

    def begin(k):
        pieces = [r_outer[views - 2], r_outer[views - 1]] + r_mid[1:] + r_last
        sent(pieces[k])
        start(pieces[k + 2])

    outer(0)
    mid(0)
    begin(0)
    finish(0)
    for v in range(1, views):
        outer(v)
        if v == 1:
            begin(1)
    for v in range(1, views - 1):
        mid(v)
        begin(v + 1)
        finish(v)
    for k in range(2):
        for c in r_last[k]:
            c.wait_recv()
        backward_z(views - 1, PAD + k * inner // 2, inner // 2)
    for c in c_y[views - 1]:
        c.wait_recv()

    per = depth // PARTS
    exchange = []
    for k in range(PARTS):
        correction(views - 1, k * per, per)
        slot = next(slots)
        part = pltpu.make_async_remote_copy(
            src_ref=acc.at[pl.ds(k * per, per)], dst_ref=other.at[pl.ds(k * per, per)],
            send_sem=send.at[slot], recv_sem=recv.at[slot],
            device_id={"view": 1 - ci}, device_id_type=pl.DeviceIdType.MESH)
        part.start()
        exchange.append(part)
    for k, part in enumerate(exchange):
        part.wait_recv()

        def step(z, carry):
            out[z] = fpad[PAD + z, pl.ds(PAD, height), :] * (acc[z] * other[z])
            return carry
        lax.fori_loop(k * per, (k + 1) * per, step, 0)

    for c in f_z[0] + f_z[1] + f_s[0] + f_s[1] + f_y:
        c.wait_send()
    for zs, _ in sides:
        @pl.when(has["gz", -zs])
        def _(zs=zs):
            for c in f_c[zs]:
                c.wait_send()
    for k in range(2):
        sent(r_last[k])
    for v in range(views):
        sent(c_y[v])
    for part in exchange:
        part.wait_send()


def solution(mesh):
    zpeers, ypeers = mesh.shape["gz"], mesh.shape["gy"]

    def body(images, estimate, psf, coverage):
        views, depth, height, width = images.shape
        zext, yext = depth + 2 * PAD, height + 2 * PAD
        f32, bf16 = jnp.float32, jnp.bfloat16
        return pl.pallas_call(
            functools.partial(kernel, images.shape, zpeers, ypeers),
            out_shape=pltpu.VMEM(estimate.shape, f32),
            in_specs=[
                pl.BlockSpec(memory_space=pltpu.SMEM),
                pl.BlockSpec(memory_space=pltpu.SMEM),
                pl.BlockSpec(memory_space=pl.ANY),
                pl.BlockSpec(memory_space=pl.ANY),
            ],
            out_specs=pl.BlockSpec(memory_space=pltpu.VMEM),
            scratch_shapes=[
                pltpu.VMEM((zext, yext, width), f32),
                pltpu.VMEM((views * depth, yext, width), f32),
                pltpu.VMEM(images.shape, f32),
                pltpu.VMEM((views, zext, height, width), f32),
                pltpu.VMEM((views, depth, yext, width), f32),
                pltpu.VMEM(estimate.shape, f32),
                pltpu.VMEM(estimate.shape, f32),
                pltpu.VMEM((2 * views * depth, 2 * zext), bf16),
                pltpu.VMEM((views, 2 * depth, 2 * zext), bf16),
                pltpu.VMEM((views, 2 * height, 2 * yext), bf16),
                pltpu.VMEM((views, 2 * height, 2 * yext), bf16),
                pltpu.VMEM((2 * (height - 2 * PAD), 2 * height), bf16),
                pltpu.VMEM((2 * PAD, 6 * PAD), bf16),
                pltpu.VMEM((views, 2 * width, 2 * width), bf16),
                pltpu.VMEM((views, 2 * width, 2 * width), bf16),
                pltpu.SemaphoreType.DMA((64,)),
                pltpu.SemaphoreType.DMA((64,)),
                pltpu.SemaphoreType.DMA((2,)),
            ],
            compiler_params=pltpu.CompilerParams(
                collective_id=0, has_side_effects=True, vmem_limit_bytes=60 * 2**20),
        )(psf, coverage.reshape(views), images, estimate)

    return jax.shard_map(
        body,
        mesh=mesh,
        in_specs=(
            P("view", ("tile", "gz"), "gy", None),
            P(("tile", "gz"), "gy", None),
            P("view", None, None),
            P("view", ("tile", "gz"), "gy"),
        ),
        out_specs=P(("tile", "gz"), "gy", None),
        check_vma=False,
    )
```
